128 devices in a mesh: dp: 16 (over x, z), tensor: 8 (over y, core).
Axes of the slice: x: 4, y: 4, z: 4, core: 2. Of those that a mesh axis runs over, the one named last changes fastest.
Arguments:
- normed_input: bfloat16 [16384, 6144], P('dp'), may hold values from -120 to 120
- query_grad: bfloat16 [16384, 6144], P('dp', 'tensor'), may hold values from -45 to 45
- query_weight: bfloat16 [6144, 6144], P('dp', 'tensor'), may hold values from -0.078125 to 0.078125
Outputs:
- input_grad: bfloat16 [16384, 6144], P('dp', 'tensor')
- weight_grad: float32 [6144, 6144], P('dp', 'tensor')
- grad_peak: float32 [], replicated
The draws below stay inside these ranges and needn't reach their ends.
All inputs are finite; a program needn't handle non-finite values.
Results may differ from the reference program's by a relative error of at most 0.02.
Values may be sent and summed in bfloat16 or wider, within the bound.
No kernel may reach another device: no remote copies, remote signals or barrier semaphores. Data moves between devices by JAX's collectives and lax.ppermute only.
A program may use at most 192 MiB of HBM per device.

```python
import math
import jax
import jax.numpy as jnp
from jax import lax

D = 6144
TOK_DEV = 1024
HQ = 6144
TOKENS = 16384
N_DP = 16
N_TENSOR = 8


def draw_normed_input(key, part):
    key = jax.random.fold_in(key, 11)
    first, second, third = jax.random.split(key, 3)
    trend = 3.0
    base = jnp.clip(jax.random.normal(first, (TOKENS, D), jnp.float32), -4.0, 4.0)
    ramp = jnp.exp(math.log(trend) * jnp.arange(TOKENS, dtype=jnp.float32) / TOKENS)
    rows = jnp.exp(jax.random.uniform(second, (TOKENS,), jnp.float32) * math.log(10.0)) * ramp
    feats = jnp.exp(jax.random.uniform(third, (D,), jnp.float32) * math.log(10.0))
    return (base * rows[:, None] * feats[None, :] / 30.0).astype(jnp.bfloat16)


def draw_query_grad(key, part):
    key = jax.random.fold_in(key, 23)
    first, second = jax.random.split(key, 2)
    trend = 3.0
    base = jnp.clip(jax.random.normal(first, (TOKENS, HQ), jnp.float32), -4.0, 4.0)
    ramp = jnp.exp(math.log(trend) * jnp.arange(HQ, dtype=jnp.float32) / HQ)
    columns = jnp.exp(jax.random.uniform(second, (HQ,), jnp.float32) * math.log(10.0)) * ramp
    return (base * columns[None, :] / 8.0).astype(jnp.bfloat16)


def level_of(key, dims, cuts, least, high):
    loudness = 1.0
    for dim, parts in cuts:
        steps = jax.random.uniform(jax.random.fold_in(jax.random.fold_in(key, 6), dim), (parts,), jnp.float32, least / len(cuts), high / len(cuts))
        loudness = loudness * jnp.repeat(jnp.exp(steps), dims[dim] // parts).reshape((-1,) + (1,) * (len(dims) - 1 - dim))
    return loudness


def scatter_about(own_key, extent, deviation, bound, shards=(), held_as=jnp.bfloat16):
    values = deviation * jax.random.normal(own_key, extent, jnp.float32)
    if shards:
        values = values * level_of(own_key, extent, shards, -0.22, 0.18)
    return jnp.clip(values, -bound, bound).astype(held_as)


def setup_inputs(seed: int = 0) -> dict:
    streams_of = jax.random.split(jax.random.key(seed), 4)
    return {
        "normed_input": draw_normed_input(jax.random.fold_in(streams_of[3], 71), 0),
        "query_grad": draw_query_grad(jax.random.fold_in(streams_of[3], 71), 0),
        "query_weight": scatter_about(streams_of[2], (D, HQ), D ** -0.5, 0.078125, ((0, 16), (1, 8))),
    }


def replica_product(inputs, grads):
    return jnp.dot(inputs.T, grads, preferred_element_type=jnp.float32)


def reference(normed_input, query_grad, query_weight):
    inputs3 = normed_input.reshape(N_DP, TOK_DEV, D)
    grads3 = query_grad.reshape(N_DP, TOK_DEV, HQ)

    def peak_step(carry, pair):
        value = replica_product(pair[0], pair[1])
        return jnp.maximum(carry, jnp.max(jnp.abs(value))), None

    grad_peak, unused = lax.scan(peak_step, jnp.zeros((), jnp.float32), (inputs3, grads3))

    def sum_step(carry, pair):
        value = replica_product(pair[0], pair[1])
        rounded = lax.optimization_barrier((value / grad_peak).astype(jnp.bfloat16))
        return carry + rounded.astype(jnp.float32), None

    weight_grad, unused2 = lax.scan(sum_step, jnp.zeros((D, HQ), jnp.float32), (inputs3, grads3))

    block_width = HQ // N_TENSOR
    grad_blocks = query_grad.reshape(TOKENS, N_TENSOR, block_width).transpose(1, 0, 2)
    weight_blocks = query_weight.reshape(D, N_TENSOR, block_width).transpose(1, 0, 2)

    def block_step(carry, pair):
        term = jnp.dot(pair[0], pair[1].T, preferred_element_type=jnp.float32)
        rounded = lax.optimization_barrier(term.astype(jnp.bfloat16))
        return carry + rounded.astype(jnp.float32), None

    summed, unused3 = lax.scan(block_step, jnp.zeros((TOKENS, D), jnp.float32), (grad_blocks, weight_blocks))
    input_grad = summed.astype(jnp.bfloat16)
    return input_grad, weight_grad, grad_peak
```

```python
import jax
import jax.numpy as jnp
import numpy as np
from jax import lax
from jax.experimental import pallas as pl
from jax.experimental.pallas import tpu as pltpu
from jax.sharding import PartitionSpec as P

F32, BF16 = jnp.float32, jnp.bfloat16
AXES = ("dp", "tensor")
NX, NY, NZ = 4, 4, 4
CHUNKS = 2


def permutation(move):
    pairs = []
    for x in range(NX):
        for z in range(NZ):
            for y in range(NY):
                for c in range(2):
                    to = move(x, y, z, c)
                    pairs.append((flat(x, y, z, c), flat(*to)))
    return pairs


def flat(x, y, z, c):
    return ((x % NX) * NZ + z % NZ) * NY * 2 + (y % NY) * 2 + c % 2


def step_along(second, d):
    def move(x, y, z, c):
        return (x + d, y, z, c) if (c ^ second) == 0 else (x, y, z + d, c)

    return permutation(move)


FIRST = {d: step_along(0, d) for d in (1, -1, 2)}
SECOND = {d: step_along(1, d) for d in (1, -1, 2)}
HAND_ON = permutation(lambda x, y, z, c: (x, y + 1 - 2 * c, z, c))
SIBLING = permutation(lambda x, y, z, c: (x, y, z, c + 1))
HALVINGS = (
    SIBLING,
    permutation(lambda x, y, z, c: (x, y + 1, z, c)),
    permutation(lambda x, y, z, c: (x, y + 2, z, c)),
    permutation(lambda x, y, z, c: (x + 1, y, z, c)),
    permutation(lambda x, y, z, c: (x + 2, y, z, c)),
    permutation(lambda x, y, z, c: (x, y, z + 1, c)),
    permutation(lambda x, y, z, c: (x, y, z + 2, c)),
)


def send(value, pairs):
    return lax.ppermute(value, AXES, pairs)


def add(*terms):
    total = terms[0].astype(F32)
    for term in terms[1:]:
        total = total + term.astype(F32)
    return total


W_ORDER = (
    [(2, 0), (2, 1), (1, 2), (1, 3)]
    + [(2, 2), (2, 3), (3, 0), (3, 1)]
    + [(1, 0), (1, 1), (3, 2), (3, 3)]
    + [(0, 0), (0, 1), (0, 2), (0, 3)]
)


def weight_kernel(order, x_ref, g_ref, plus_ref, minus_ref, rest_ref, peak_ref, gt_ref):
    n = pl.program_id(0)

    @pl.when(n == 0)
    def _():
        gt_ref[...] = g_ref[...].T
        peak_ref[...] = jnp.zeros_like(peak_ref)

    out = jnp.dot(gt_ref[...], x_ref[...], preferred_element_type=F32)
    rows, cols = out.shape
    peak_ref[...] = jnp.maximum(
        peak_ref[...], jnp.max(jnp.abs(out).reshape(rows // 8, 8, cols), axis=0)
    )
    low = out.astype(BF16)

    @pl.when(n < 4)
    def _():
        plus_ref[0] = low

    @pl.when((n >= 4) & (n < 8))
    def _():
        minus_ref[0] = low

    @pl.when(n >= 8)
    def _():
        rest_ref[0] = low


def weight_products(order, base, x, g):
    tokens, d = x.shape
    cols = g.shape[1]
    rows = d // 16
    grid_spec = pltpu.PrefetchScalarGridSpec(
        num_scalar_prefetch=1,
        grid=(16,),
        in_specs=[
            pl.BlockSpec((tokens, rows), lambda n, o: (0, o[base + n])),
            pl.BlockSpec((tokens, cols), lambda n, o: (0, 0)),
        ],
        out_specs=[
            pl.BlockSpec((1, cols, rows), lambda n, o: (jnp.minimum(n, 3), 0, 0)),
            pl.BlockSpec((1, cols, rows), lambda n, o: (jnp.clip(n - 4, 0, 3), 0, 0)),
            pl.BlockSpec((1, cols, rows), lambda n, o: (jnp.maximum(n - 8, 0), 0, 0)),
            pl.BlockSpec((8, rows), lambda n, o: (0, 0)),
        ],
        scratch_shapes=[pltpu.VMEM((cols, tokens), BF16)],
    )
    return pl.pallas_call(
        weight_kernel,
        grid_spec=grid_spec,
        out_shape=[
            jax.ShapeDtypeStruct((4, cols, rows), BF16),
            jax.ShapeDtypeStruct((4, cols, rows), BF16),
            jax.ShapeDtypeStruct((8, cols, rows), BF16),
            jax.ShapeDtypeStruct((8, rows), F32),
        ],
        compiler_params=pltpu.CompilerParams(vmem_limit_bytes=40 * 2**20),
        cost_estimate=pl.CostEstimate(flops=1, bytes_accessed=1, transcendentals=0),
        name="weight_products",
    )(order, x, g)


def tables():
    rows = []
    for dp in range(NX * NZ):
        for t in range(NY * 2):
            x, z, y, c = dp // NZ, dp % NZ, t // 2, t % 2
            row = []
            for core in (1 - c, c):
                for d in I_DEST:
                    fx = (y + (d if c == 0 else -d)) % NY
                    for e in range(2):
                        fz = 2 * core + e
                        off_x, off_z = (x - fx) % NX, (z - fz) % NZ
                        i, j = (off_x, off_z) if c == 0 else (off_z, off_x)
                        row.append(SLOT[j] * 4 + SLOT[i])
            for first, second in W_ORDER:
                rx, rz = (first, second) if c == 0 else (second, first)
                row.append(((x + rx) % NX) * NZ + (z + rz) % NZ)
            rows.append(row)
    return np.array(rows, np.int32)


SLOT = (0, 1, 3, 2)
I_DEST = (3, 2, 1, 0)
NT = (((1,), (1,)), ((), ()))


def give_kernel(order, g_ref, w0, w1, out_ref):
    w = jnp.concatenate([w0[0], w1[0]], axis=0)
    out_ref[0] = lax.dot_general(g_ref[...], w, NT, preferred_element_type=F32).astype(BF16)


def keep_kernel(order, g_ref, w0, w1, got_ref, first_ref, rest_ref):
    n = pl.program_id(0)
    w = jnp.concatenate([w0[0], w1[0]], axis=0)
    out = lax.dot_general(g_ref[...], w, NT, preferred_element_type=F32)
    low = (out + got_ref[0].astype(F32)).astype(BF16)

    @pl.when(n == 0)
    def _():
        first_ref[0] = low

    @pl.when(n > 0)
    def _():
        rest_ref[0] = low


def input_products(order, base, g, w, got=None):
    tokens, k = g.shape
    rows = w.shape[1]
    shape = (1, tokens, 2 * rows)

    def w_spec(e):
        return pl.BlockSpec((1, rows, k), lambda n, o: (o[base + 2 * n + e], 0, 0))

    in_specs = [pl.BlockSpec((tokens, k), lambda n, o: (0, 0)), w_spec(0), w_spec(1)]
    args = [g, w, w]
    if got is None:
        out_specs = pl.BlockSpec(shape, lambda n, o: (n, 0, 0))
        out_shape = jax.ShapeDtypeStruct((4,) + shape[1:], BF16)
    else:
        in_specs.append(pl.BlockSpec(shape, lambda n, o: (jnp.where(n == 3, 3, 2 - n), 0, 0)))
        args.append(got)
        out_specs = [
            pl.BlockSpec(shape, lambda n, o: (0, 0, 0)),
            pl.BlockSpec(shape, lambda n, o: (jnp.maximum(n - 1, 0), 0, 0)),
        ]
        out_shape = [
            jax.ShapeDtypeStruct(shape, BF16),
            jax.ShapeDtypeStruct((3,) + shape[1:], BF16),
        ]
    return pl.pallas_call(
        give_kernel if got is None else keep_kernel,
        grid_spec=pltpu.PrefetchScalarGridSpec(
            num_scalar_prefetch=1, grid=(4,), in_specs=in_specs, out_specs=out_specs
        ),
        out_shape=out_shape,
        compiler_params=pltpu.CompilerParams(vmem_limit_bytes=40 * 2**20),
        cost_estimate=pl.CostEstimate(flops=1, bytes_accessed=1, transcendentals=0),
        name="give_products" if got is None else "keep_products",
    )(order, *args)


def tie_kernel(*refs):
    pass


def tie(value, *after):
    spec = pl.BlockSpec(memory_space=pl.ANY)
    return pl.pallas_call(
        tie_kernel,
        in_specs=[spec] * (1 + len(after)),
        out_specs=spec,
        out_shape=jax.ShapeDtypeStruct(value.shape, value.dtype),
        input_output_aliases={0: 0},
        cost_estimate=pl.CostEstimate(flops=1, bytes_accessed=1, transcendentals=0),
        name="tie",
    )(value, *after)


def per_device(x_in, g, w):
    dp = lax.axis_index("dp")
    t = lax.axis_index("tensor")
    table = tables()
    order = lax.dynamic_index_in_dim(jnp.asarray(table), dp * NY * 2 + t, 0, keepdims=False)

    near = [w, send(w, FIRST[1]), send(w, FIRST[-1]), send(w, FIRST[2])]
    plus, minus, rest, peak8 = weight_products(order, 16, x_in, g)
    near[3] = tie(near[3], peak8)

    part = w.shape[0] // CHUNKS
    lines = [jnp.stack([b[j * part : (j + 1) * part] for b in near]) for j in range(CHUNKS)]
    wholes = []
    for line in lines:
        up, down = send(line, SECOND[1]), send(line, SECOND[-1])
        far = [send(up[:2], SECOND[1]), send(down[2:], SECOND[-1])]
        wholes.append(jnp.concatenate([line, up, down] + far, axis=0))

    u, v = send(plus, FIRST[1]), send(minus, FIRST[-1])
    r = send(add(rest[0:2], u[0:2]).astype(BF16), FIRST[1])
    s = send(add(rest[2:4], v[0:2]).astype(BF16), FIRST[-1])
    e = [add(rest[4], v[2], r[0]), add(rest[5], v[3], r[1]), add(rest[6], u[2], s[0]), add(rest[7], u[3], s[1])]
    e = [b.astype(BF16) for b in e]
    h = e[0].shape[0] // 2
    u = send(jnp.stack([e[2][:h], e[1][h:]]), SECOND[1])
    v = send(jnp.stack([e[2][h:], e[3][:h]]), SECOND[-1])
    r = send(add(e[1][:h], u[0]).astype(BF16), SECOND[1])
    s = send(add(e[3][h:], v[0]).astype(BF16), SECOND[-1])
    total = jnp.concatenate([add(e[0][:h], v[1], r), add(e[0][h:], u[1], s)], axis=0)

    pieces = []
    for whole in wholes:
        got = send(input_products(order, 0, g, whole), SIBLING)
        first, others = input_products(order, 8, g, whole, got)
        hop = send(first[0], HAND_ON)
        hop = send(add(others[0], hop).astype(BF16), HAND_ON)
        hop = send(add(others[1], hop).astype(BF16), HAND_ON)
        pieces.append(add(others[2], hop).astype(BF16))

    peak = jnp.broadcast_to(jnp.max(peak8), (1, 128))
    for pairs in HALVINGS:
        peak = jnp.maximum(peak, send(peak, pairs))
    grad_peak = peak[0, 0]
    weight_grad = total.T / grad_peak
    input_grad = jnp.concatenate([p[:, e * part : (e + 1) * part] for e in range(2) for p in pieces], axis=1)
    return input_grad, weight_grad, grad_peak


def solution(mesh):
    return jax.shard_map(
        per_device,
        mesh=mesh,
        in_specs=(P("dp", None), P("dp", "tensor"), P("dp", "tensor")),
        out_specs=(P("dp", "tensor"), P("dp", "tensor"), P()),
        check_vma=False,
    )
```

```python
import jax
import jax.numpy as jnp
import numpy as np
from jax import lax
from jax.experimental import pallas as pl
from jax.experimental.pallas import tpu as pltpu
from jax.sharding import PartitionSpec as P

F32, BF16 = jnp.float32, jnp.bfloat16
AXES = ("dp", "tensor")
NX, NY, NZ = 4, 4, 4


def permutation(move):
    pairs = []
    for x in range(NX):
        for z in range(NZ):
            for y in range(NY):
                for c in range(2):
                    to = move(x, y, z, c)
                    pairs.append((flat(x, y, z, c), flat(*to)))
    return pairs


def flat(x, y, z, c):
    return ((x % NX) * NZ + z % NZ) * NY * 2 + (y % NY) * 2 + c % 2


def step_along(second, d):
    def move(x, y, z, c):
        return (x + d, y, z, c) if (c ^ second) == 0 else (x, y, z + d, c)

    return permutation(move)


FIRST = {d: step_along(0, d) for d in (1, -1, 2)}
SECOND = {d: step_along(1, d) for d in (1, -1, 2)}
TURN = permutation(lambda x, y, z, c: (x + y, x, 2 * c + z % 2, z // 2))


def send(value, pairs):
    return lax.ppermute(value, AXES, pairs)


def add(*terms):
    total = terms[0].astype(F32)
    for term in terms[1:]:
        total = total + term.astype(F32)
    return total


W_ORDER = (
    [(2, 0), (2, 1), (1, 2), (1, 3)]
    + [(2, 2), (2, 3), (3, 0), (3, 1)]
    + [(1, 0), (1, 1), (3, 2), (3, 3)]
    + [(0, 0), (0, 1), (0, 2), (0, 3)]
)


def weight_kernel(order, x_ref, g_ref, *refs):
    *out_refs, peak_ref, gt_ref = refs
    n = pl.program_id(0)

    @pl.when(n == 0)
    def _():
        gt_ref[...] = g_ref[...].T
        peak_ref[...] = jnp.zeros_like(peak_ref)

    out = jnp.dot(gt_ref[...], x_ref[...], preferred_element_type=F32)
    rows, cols = out.shape
    peak_ref[...] = jnp.maximum(
        peak_ref[...], jnp.max(jnp.abs(out).reshape(rows // 8, 8, cols), axis=0)
    )
    low = out.astype(BF16)
    for i, out_ref in enumerate(out_refs):

        @pl.when(n // 4 == i)
        def _(out_ref=out_ref):
            out_ref[0] = low


def weight_products(order, base, arrays, x, g):
    tokens, d = x.shape
    cols = g.shape[1]
    rows = d // (NX * NZ)
    grid_spec = pltpu.PrefetchScalarGridSpec(
        num_scalar_prefetch=1,
        grid=(4 * arrays,),
        in_specs=[
            pl.BlockSpec((tokens, rows), lambda n, o: (0, o[base + n])),
            pl.BlockSpec((tokens, cols), lambda n, o: (0, 0)),
        ],
        out_specs=[
            pl.BlockSpec((1, cols, rows), lambda n, o, i=i: (jnp.clip(n - 4 * i, 0, 3), 0, 0))
            for i in range(arrays)
        ]
        + [pl.BlockSpec((8, rows), lambda n, o: (0, 0))],
        scratch_shapes=[pltpu.VMEM((cols, tokens), BF16)],
    )
    return pl.pallas_call(
        weight_kernel,
        grid_spec=grid_spec,
        out_shape=[jax.ShapeDtypeStruct((4, cols, rows), BF16)] * arrays
        + [jax.ShapeDtypeStruct((8, rows), F32)],
        compiler_params=pltpu.CompilerParams(vmem_limit_bytes=40 * 2**20),
        cost_estimate=pl.CostEstimate(
            flops=2 * tokens * cols * rows * 4 * arrays, bytes_accessed=2 * 4 * arrays * rows * (tokens + cols), transcendentals=0
        ),
        name="weight_products",
    )(order, x, g)


SLOTS = (0, 1, 3, 2)


def tables():
    rows = []
    for dp in range(NX * NZ):
        for t in range(NY * 2):
            x, z, y, c = dp // NZ, dp % NZ, t // 2, t % 2
            columns, halves, row = [], [], []
            for j in SLOTS:
                for i in SLOTS:
                    bx, bz = ((x - i) % NX, (z - j) % NZ) if c == 0 else ((x - j) % NX, (z - i) % NZ)
                    columns.append(2 * ((bx - y) % NY) + bz // 2)
                    halves.append(bz % 2)
            for first, second in W_ORDER:
                rx, rz = (first, second) if c == 0 else (second, first)
                row.append(((x + rx) % NX) * NZ + (z + rz) % NZ)
            rows.append(columns + halves + row)
    return np.array(rows, np.int32)


BLOCKS = NX * NZ
W_BASE = 2 * BLOCKS


def block_product(g_ref, w_refs, per_array):
    n = pl.program_id(0)
    w = w_refs[0][0]
    for q in range(1, len(w_refs)):
        w = jnp.where(n >= q * per_array, w_refs[q][0], w)
    return lax.dot_general(g_ref[0], w, (((1,), (1,)), ((), ())), preferred_element_type=F32)


def begin_kernel(order, g_ref, w0, w1, w2, sum_ref):
    n = pl.program_id(0)

    @pl.when(n == 0)
    def _():
        sum_ref[...] = jnp.zeros_like(sum_ref)

    sum_ref[order[BLOCKS + n]] += block_product(g_ref, (w0, w1, w2), 4)


def end_kernel(order, g_ref, w0, w1, begun_ref, out_ref, sum_ref):
    n = pl.program_id(0)

    @pl.when(n == 0)
    def _():
        sum_ref[...] = begun_ref[...]

    sum_ref[order[BLOCKS + 12 + n]] += block_product(g_ref, (w0, w1), 2)

    @pl.when(n == pl.num_programs(0) - 1)
    def _():
        half = sum_ref.shape[2]
        out_ref[:, :half] = sum_ref[0].astype(BF16)
        out_ref[:, half:] = sum_ref[1].astype(BF16)


def input_products(order, g, arrays, begun=None):
    tokens, k = g.shape[1:]
    per_array, rows = arrays[0].shape[:2]
    steps = per_array * len(arrays)
    first = 0 if begun is None else 12
    whole = (2, tokens, rows)
    in_specs = [pl.BlockSpec((1, tokens, k), lambda n, o: (o[first + n], 0, 0))]
    in_specs += [
        pl.BlockSpec((1, rows, k), lambda n, o, q=q: (jnp.clip(n - q * per_array, 0, per_array - 1), 0, 0))
        for q in range(len(arrays))
    ]
    args = [g, *arrays]
    if begun is None:
        out_specs = pl.BlockSpec(whole, lambda n, o: (0, 0, 0))
        out_shape = jax.ShapeDtypeStruct(whole, F32)
        scratch = []
    else:
        in_specs.append(pl.BlockSpec(whole, lambda n, o: (0, 0, 0)))
        args.append(begun)
        out_specs = pl.BlockSpec((tokens, 2 * rows), lambda n, o: (0, 0))
        out_shape = jax.ShapeDtypeStruct((tokens, 2 * rows), BF16)
        scratch = [pltpu.VMEM(whole, F32)]
    return pl.pallas_call(
        begin_kernel if begun is None else end_kernel,
        grid_spec=pltpu.PrefetchScalarGridSpec(
            num_scalar_prefetch=1, grid=(steps,), in_specs=in_specs, out_specs=out_specs, scratch_shapes=scratch
        ),
        out_shape=out_shape,
        compiler_params=pltpu.CompilerParams(vmem_limit_bytes=40 * 2**20),
        cost_estimate=pl.CostEstimate(
            flops=2 * steps * tokens * k * rows, bytes_accessed=2 * steps * k * (tokens + rows), transcendentals=0
        ),
        name="input_products",
    )(order, *args)


def tie_kernel(*refs):
    pass


def tie(value, *after):
    spec = pl.BlockSpec(memory_space=pl.ANY)
    return pl.pallas_call(
        tie_kernel,
        in_specs=[spec] * (1 + len(after)),
        out_specs=spec,
        out_shape=jax.ShapeDtypeStruct(value.shape, value.dtype),
        input_output_aliases={0: 0},
        cost_estimate=pl.CostEstimate(flops=1, bytes_accessed=1, transcendentals=0),
        name="tie",
    )(value, *after)


def per_device(x_in, g, w):
    dp = lax.axis_index("dp")
    t = lax.axis_index("tensor")
    table = tables()
    order = lax.dynamic_index_in_dim(jnp.asarray(table), dp * NY * 2 + t, 0, keepdims=False)

    turned = send(w, TURN)
    plus, peak_a = weight_products(order, W_BASE, 1, x_in, g)
    turned = tie(turned, peak_a)
    near = [turned, send(turned, FIRST[1]), send(turned, FIRST[-1]), send(turned, FIRST[2])]
    minus, peak_b = weight_products(order, W_BASE + 4, 1, x_in, g)
    low, high, peak_c = weight_products(order, W_BASE + 8, 2, x_in, g)
    near[3] = tie(near[3], peak_c)

    g_all = lax.all_gather(g, "tensor", axis=0)

    line = jnp.stack(near)
    up, down = send(line, SECOND[1]), send(line, SECOND[-1])
    u, v = send(plus, FIRST[1]), send(minus, FIRST[-1])

    peaks = lax.all_gather(jnp.maximum(jnp.maximum(peak_a, peak_b), peak_c), AXES)
    u = tie(u, up, down)

    far = [send(up[:2], SECOND[1]), send(down[2:], SECOND[-1])]
    r = send(add(low[0:2], u[0:2]).astype(BF16), FIRST[1])
    s = send(add(low[2:4], v[0:2]).astype(BF16), FIRST[-1])
    begun = input_products(order, g_all, [line, up, down])
    r = tie(r, begun, *far)

    e = [add(high[0], v[2], r[0]), add(high[1], v[3], r[1]), add(high[2], u[2], s[0]), add(high[3], u[3], s[1])]
    e = [b.astype(BF16) for b in e]
    h = e[0].shape[0] // 2
    u = send(jnp.stack([e[2][:h], e[1][h:]]), SECOND[1])
    v = send(jnp.stack([e[2][h:], e[3][:h]]), SECOND[-1])
    grad_peak = jnp.max(peaks)
    input_grad = input_products(order, g_all, far, begun)
    u = tie(u, input_grad, peaks)
    r = send(add(e[1][:h], u[0]).astype(BF16), SECOND[1])
    s = send(add(e[3][h:], v[0]).astype(BF16), SECOND[-1])
    total = jnp.concatenate([add(e[0][:h], v[1], r), add(e[0][h:], u[1], s)], axis=0)
    weight_grad = total.T / grad_peak
    return input_grad, weight_grad, grad_peak


def solution(mesh):
    return jax.shard_map(
        per_device,
        mesh=mesh,
        in_specs=(P("dp", None), P("dp", "tensor"), P("dp", "tensor")),
        out_specs=(P("dp", "tensor"), P("dp", "tensor"), P()),
        check_vma=False,
    )
```

```python
import functools

import jax
import jax.numpy as jnp
import numpy as np
from jax import lax
from jax.experimental import pallas as pl
from jax.experimental.pallas import tpu as pltpu
from jax.sharding import PartitionSpec as P

F32, BF16 = jnp.float32, jnp.bfloat16
AXES = ("dp", "tensor")
NX, NY, NZ = 4, 4, 4


def permutation(move):
    pairs = []
    for x in range(NX):
        for z in range(NZ):
            for y in range(NY):
                for c in range(2):
                    to = move(x, y, z, c)
                    pairs.append((flat(x, y, z, c), flat(*to)))
    return pairs


def flat(x, y, z, c):
    return ((x % NX) * NZ + z % NZ) * NY * 2 + (y % NY) * 2 + c % 2


def step_along(second, d):
    def move(x, y, z, c):
        return (x + d, y, z, c) if (c ^ second) == 0 else (x, y, z + d, c)

    return permutation(move)


FIRST = {d: step_along(0, d) for d in (1, -1, 2)}
SECOND = {d: step_along(1, d) for d in (1, -1, 2)}
TURN = permutation(lambda x, y, z, c: (x + y, x, 2 * c + z % 2, z // 2))


def send(value, pairs):
    return lax.ppermute(value, AXES, pairs)


def add(*terms):
    total = terms[0].astype(F32)
    for term in terms[1:]:
        total = total + term.astype(F32)
    return total


W_ORDER = (
    [(2, 0), (2, 1), (1, 2), (1, 3)]
    + [(2, 2), (2, 3), (3, 0), (3, 1)]
    + [(1, 0), (1, 1), (3, 2), (3, 3)]
    + [(0, 0), (0, 1), (0, 2), (0, 3)]
)


def weight_kernel(order, x_ref, g_ref, *refs):
    *out_refs, peak_ref, gt_ref = refs
    n = pl.program_id(0)

    @pl.when(n == 0)
    def _():
        gt_ref[...] = g_ref[...].T
        peak_ref[...] = jnp.zeros_like(peak_ref)

    out = jnp.dot(gt_ref[...], x_ref[...], preferred_element_type=F32)
    rows, cols = out.shape
    peak_ref[...] = jnp.maximum(
        peak_ref[...], jnp.max(jnp.abs(out).reshape(rows // 8, 8, cols), axis=0)
    )
    low = out.astype(BF16)
    for i, out_ref in enumerate(out_refs):

        @pl.when(n // 4 == i)
        def _(out_ref=out_ref):
            out_ref[0] = low


def weight_products(order, base, arrays, x, g):
    tokens, d = x.shape
    cols = g.shape[1]
    rows = d // (NX * NZ)
    grid_spec = pltpu.PrefetchScalarGridSpec(
        num_scalar_prefetch=1,
        grid=(4 * arrays,),
        in_specs=[
            pl.BlockSpec((tokens, rows), lambda n, o: (0, o[base + n])),
            pl.BlockSpec((tokens, cols), lambda n, o: (0, 0)),
        ],
        out_specs=[
            pl.BlockSpec((1, cols, rows), lambda n, o, i=i: (jnp.clip(n - 4 * i, 0, 3), 0, 0))
            for i in range(arrays)
        ]
        + [pl.BlockSpec((8, rows), lambda n, o: (0, 0))],
        scratch_shapes=[pltpu.VMEM((cols, tokens), BF16)],
    )
    return pl.pallas_call(
        weight_kernel,
        grid_spec=grid_spec,
        out_shape=[jax.ShapeDtypeStruct((4, cols, rows), BF16)] * arrays
        + [jax.ShapeDtypeStruct((8, rows), F32)],
        compiler_params=pltpu.CompilerParams(vmem_limit_bytes=40 * 2**20),
        cost_estimate=pl.CostEstimate(
            flops=2 * tokens * cols * rows * 4 * arrays, bytes_accessed=2 * 4 * arrays * rows * (tokens + cols), transcendentals=0
        ),
        name="weight_products",
    )(order, x, g)


SLOTS = (0, 1, 3, 2)


def tables():
    rows = []
    for dp in range(NX * NZ):
        for t in range(NY * 2):
            x, z, y, c = dp // NZ, dp % NZ, t // 2, t % 2
            columns, halves, row = [], [], []
            for j in SLOTS:
                for i in SLOTS:
                    bx, bz = ((x - i) % NX, (z - j) % NZ) if c == 0 else ((x - j) % NX, (z - i) % NZ)
                    columns.append(2 * ((bx - y) % NY) + bz // 2)
                    halves.append(bz % 2)
            for first, second in W_ORDER:
                rx, rz = (first, second) if c == 0 else (second, first)
                row.append(((x + rx) % NX) * NZ + (z + rz) % NZ)
            rows.append(columns + halves + row)
    return np.array(rows, np.int32)


BLOCKS = NX * NZ
W_BASE = 2 * BLOCKS


def block_product(g_ref, w_refs, per_array):
    n = pl.program_id(0)
    w = w_refs[0][0]
    for q in range(1, len(w_refs)):
        w = jnp.where(n >= q * per_array, w_refs[q][0], w)
    return lax.dot_general(g_ref[0], w, (((1,), (1,)), ((), ())), preferred_element_type=F32)


def input_kernel(first, last, order, g_ref, *refs):
    n = pl.program_id(0)
    sum_ref = refs[-1]
    if first == 0:
        w_refs = refs[:-1]

        @pl.when(n == 0)
        def _():
            sum_ref[...] = jnp.zeros_like(sum_ref)

    else:
        w_refs, begun_ref = refs[: -3 if last else -2], refs[-3 if last else -2]

        @pl.when(n == 0)
        def _():
            sum_ref[...] = begun_ref[...]

    per_array = 2 if last else 4
    sum_ref[order[BLOCKS + first + n]] += block_product(g_ref, w_refs, per_array)

    if last:
        out_ref = refs[-2]

        @pl.when(n == pl.num_programs(0) - 1)
        def _():
            half = sum_ref.shape[2]
            out_ref[:, :half] = sum_ref[0].astype(BF16)
            out_ref[:, half:] = sum_ref[1].astype(BF16)


def input_products(order, first, g, arrays, begun=None):
    tokens, k = g.shape[1:]
    per_array, rows = arrays[0].shape[:2]
    steps = per_array * len(arrays)
    last = first + steps == BLOCKS
    whole = (2, tokens, rows)
    in_specs = [pl.BlockSpec((1, tokens, k), lambda n, o: (o[first + n], 0, 0))]
    in_specs += [
        pl.BlockSpec((1, rows, k), lambda n, o, q=q: (jnp.clip(n - q * per_array, 0, per_array - 1), 0, 0))
        for q in range(len(arrays))
    ]
    args = [g, *arrays]
    if begun is not None:
        in_specs.append(pl.BlockSpec(whole, lambda n, o: (0, 0, 0)))
        args.append(begun)
    if last:
        out_specs = pl.BlockSpec((tokens, 2 * rows), lambda n, o: (0, 0))
        out_shape = jax.ShapeDtypeStruct((tokens, 2 * rows), BF16)
    else:
        out_specs = pl.BlockSpec(whole, lambda n, o: (0, 0, 0))
        out_shape = jax.ShapeDtypeStruct(whole, F32)
    return pl.pallas_call(
        functools.partial(input_kernel, first, last),
        grid_spec=pltpu.PrefetchScalarGridSpec(
            num_scalar_prefetch=1,
            grid=(steps,),
            in_specs=in_specs,
            out_specs=out_specs,
            scratch_shapes=[pltpu.VMEM(whole, F32)] if last else [],
        ),
        out_shape=out_shape,
        compiler_params=pltpu.CompilerParams(vmem_limit_bytes=40 * 2**20),
        cost_estimate=pl.CostEstimate(
            flops=2 * steps * tokens * k * rows, bytes_accessed=2 * steps * k * (tokens + rows), transcendentals=0
        ),
        name="input_products",
    )(order, *args)


def tie_kernel(*refs):
    pass


def tie(value, *after):
    spec = pl.BlockSpec(memory_space=pl.ANY)
    return pl.pallas_call(
        tie_kernel,
        in_specs=[spec] * (1 + len(after)),
        out_specs=spec,
        out_shape=jax.ShapeDtypeStruct(value.shape, value.dtype),
        input_output_aliases={0: 0},
        cost_estimate=pl.CostEstimate(flops=1, bytes_accessed=1, transcendentals=0),
        name="tie",
    )(value, *after)


def per_device(x_in, g, w):
    dp = lax.axis_index("dp")
    t = lax.axis_index("tensor")
    table = tables()
    order = lax.dynamic_index_in_dim(jnp.asarray(table), dp * NY * 2 + t, 0, keepdims=False)

    turned = send(w, TURN)
    plus, peak_a = weight_products(order, W_BASE, 1, x_in, g)
    turned = tie(turned, peak_a)
    near = [turned, send(turned, FIRST[1]), send(turned, FIRST[-1]), send(turned, FIRST[2])]
    minus, peak_b = weight_products(order, W_BASE + 4, 1, x_in, g)
    low, high, peak_c = weight_products(order, W_BASE + 8, 2, x_in, g)
    near[3] = tie(near[3], peak_c)

    g_all = lax.all_gather(g, "tensor", axis=0)

    line = jnp.stack(near)
    up, down = send(line, SECOND[1]), send(line, SECOND[-1])
    u, v = send(plus, FIRST[1]), send(minus, FIRST[-1])

    begun = input_products(order, 0, g_all, [line])
    peaks = lax.all_gather(tie(jnp.maximum(jnp.maximum(peak_a, peak_b), peak_c), begun), AXES)
    u = tie(u, up, down)

    far = [send(up[:2], SECOND[1]), send(down[2:], SECOND[-1])]
    r = send(add(low[0:2], u[0:2]).astype(BF16), FIRST[1])
    s = send(add(low[2:4], v[0:2]).astype(BF16), FIRST[-1])
    begun = input_products(order, 4, g_all, [up, down], begun)
    r = tie(r, begun, *far)

    e = [add(high[0], v[2], r[0]), add(high[1], v[3], r[1]), add(high[2], u[2], s[0]), add(high[3], u[3], s[1])]
    e = [b.astype(BF16) for b in e]
    h = e[0].shape[0] // 2
    u = send(jnp.stack([e[2][:h], e[1][h:]]), SECOND[1])
    v = send(jnp.stack([e[2][h:], e[3][:h]]), SECOND[-1])
    grad_peak = jnp.max(peaks)
    input_grad = input_products(order, 12, g_all, far, begun)
    u = tie(u, input_grad, peaks)
    r = send(add(e[1][:h], u[0]).astype(BF16), SECOND[1])
    s = send(add(e[3][h:], v[0]).astype(BF16), SECOND[-1])
    total = jnp.concatenate([add(e[0][:h], v[1], r), add(e[0][h:], u[1], s)], axis=0)
    weight_grad = total.T / grad_peak
    return input_grad, weight_grad, grad_peak


def solution(mesh):
    return jax.shard_map(
        per_device,
        mesh=mesh,
        in_specs=(P("dp", None), P("dp", "tensor"), P("dp", "tensor")),
        out_specs=(P("dp", "tensor"), P("dp", "tensor"), P()),
        check_vma=False,
    )
```

```python
import jax
import jax.numpy as jnp
import numpy as np
from jax import lax
from jax.experimental import pallas as pl
from jax.experimental.pallas import tpu as pltpu
from jax.sharding import PartitionSpec as P

F32, BF16 = jnp.float32, jnp.bfloat16
AXES = ("dp", "tensor")
NX, NY, NZ = 4, 4, 4


def permutation(move):
    pairs = []
    for x in range(NX):
        for z in range(NZ):
            for y in range(NY):
                for c in range(2):
                    to = move(x, y, z, c)
                    pairs.append((flat(x, y, z, c), flat(*to)))
    return pairs


def flat(x, y, z, c):
    return ((x % NX) * NZ + z % NZ) * NY * 2 + (y % NY) * 2 + c % 2


def step_along(second, d):
    def move(x, y, z, c):
        return (x + d, y, z, c) if (c ^ second) == 0 else (x, y, z + d, c)

    return permutation(move)


FIRST = {d: step_along(0, d) for d in (1, -1, 2)}
SECOND = {d: step_along(1, d) for d in (1, -1, 2)}
TURN = permutation(lambda x, y, z, c: (x + y, x, 2 * c + z % 2, z // 2))


def send(value, pairs):
    return lax.ppermute(value, AXES, pairs)


def add(*terms):
    total = terms[0].astype(F32)
    for term in terms[1:]:
        total = total + term.astype(F32)
    return total


W_ORDER = (
    [(2, 0), (2, 1), (1, 2), (1, 3)]
    + [(2, 2), (2, 3), (3, 0), (3, 1)]
    + [(1, 0), (1, 1), (3, 2), (3, 3)]
    + [(0, 0), (0, 1), (0, 2), (0, 3)]
)


def weight_kernel(order, x_ref, g_ref, *refs):
    *out_refs, peak_ref, gt_ref = refs
    n = pl.program_id(0)

    @pl.when(n == 0)
    def _():
        gt_ref[...] = g_ref[...].T
        peak_ref[...] = jnp.zeros_like(peak_ref)

    out = jnp.dot(gt_ref[...], x_ref[...], preferred_element_type=F32)
    rows, cols = out.shape
    peak_ref[...] = jnp.maximum(
        peak_ref[...], jnp.max(jnp.abs(out).reshape(rows // 8, 8, cols), axis=0)
    )
    low = out.astype(BF16)
    for i, out_ref in enumerate(out_refs):

        @pl.when(n // 4 == i)
        def _(out_ref=out_ref):
            out_ref[0] = low


def weight_products(order, base, arrays, x, g):
    tokens, d = x.shape
    cols = g.shape[1]
    rows = d // (NX * NZ)
    grid_spec = pltpu.PrefetchScalarGridSpec(
        num_scalar_prefetch=1,
        grid=(4 * arrays,),
        in_specs=[
            pl.BlockSpec((tokens, rows), lambda n, o: (0, o[base + n])),
            pl.BlockSpec((tokens, cols), lambda n, o: (0, 0)),
        ],
        out_specs=[
            pl.BlockSpec((1, cols, rows), lambda n, o, i=i: (jnp.clip(n - 4 * i, 0, 3), 0, 0))
            for i in range(arrays)
        ]
        + [pl.BlockSpec((8, rows), lambda n, o: (0, 0))],
        scratch_shapes=[pltpu.VMEM((cols, tokens), BF16)],
    )
    return pl.pallas_call(
        weight_kernel,
        grid_spec=grid_spec,
        out_shape=[jax.ShapeDtypeStruct((4, cols, rows), BF16)] * arrays
        + [jax.ShapeDtypeStruct((8, rows), F32)],
        compiler_params=pltpu.CompilerParams(vmem_limit_bytes=40 * 2**20),
        cost_estimate=pl.CostEstimate(
            flops=2 * tokens * cols * rows * 4 * arrays, bytes_accessed=2 * 4 * arrays * rows * (tokens + cols), transcendentals=0
        ),
        name="weight_products",
    )(order, x, g)


SLOTS = (0, 1, 3, 2)


def tables():
    rows = []
    for dp in range(NX * NZ):
        for t in range(NY * 2):
            x, z, y, c = dp // NZ, dp % NZ, t // 2, t % 2
            columns, halves, row = [], [], []
            for j in SLOTS:
                for i in SLOTS:
                    bx, bz = ((x - i) % NX, (z - j) % NZ) if c == 0 else ((x - j) % NX, (z - i) % NZ)
                    columns.append(2 * ((bx - y) % NY) + bz // 2)
                    halves.append(bz % 2)
            for first, second in W_ORDER:
                rx, rz = (first, second) if c == 0 else (second, first)
                row.append(((x + rx) % NX) * NZ + (z + rz) % NZ)
            rows.append(columns + halves + row)
    return np.array(rows, np.int32)


BLOCKS = NX * NZ
W_BASE = 2 * BLOCKS


def add_product(sum_ref, half, g_ref, w_refs, per_array):
    n = pl.program_id(0)
    for q, w_ref in enumerate(w_refs):

        @pl.when(n // per_array == q)
        def _(w_ref=w_ref):
            sum_ref[half] += lax.dot_general(
                g_ref[0], w_ref[0], (((1,), (1,)), ((), ())), preferred_element_type=F32
            )


def begin_kernel(order, g_ref, w0, w1, w2, sum_ref):
    n = pl.program_id(0)

    @pl.when(n == 0)
    def _():
        sum_ref[...] = jnp.zeros_like(sum_ref)

    add_product(sum_ref, order[BLOCKS + n], g_ref, (w0, w1, w2), 4)


def end_kernel(order, g_ref, w0, w1, begun_ref, out_ref, sum_ref):
    n = pl.program_id(0)

    @pl.when(n == 0)
    def _():
        sum_ref[...] = begun_ref[...]

    add_product(sum_ref, order[BLOCKS + 12 + n], g_ref, (w0, w1), 2)

    @pl.when(n == pl.num_programs(0) - 1)
    def _():
        half = sum_ref.shape[2]
        out_ref[:, :half] = sum_ref[0].astype(BF16)
        out_ref[:, half:] = sum_ref[1].astype(BF16)


def input_products(order, g, arrays, begun=None):
    tokens, k = g.shape[1:]
    per_array, rows = arrays[0].shape[:2]
    steps = per_array * len(arrays)
    first = 0 if begun is None else 12
    whole = (2, tokens, rows)
    in_specs = [pl.BlockSpec((1, tokens, k), lambda n, o: (o[first + n], 0, 0))]
    in_specs += [
        pl.BlockSpec((1, rows, k), lambda n, o, q=q: (jnp.clip(n - q * per_array, 0, per_array - 1), 0, 0))
        for q in range(len(arrays))
    ]
    args = [g, *arrays]
    if begun is None:
        out_specs = pl.BlockSpec(whole, lambda n, o: (0, 0, 0))
        out_shape = jax.ShapeDtypeStruct(whole, F32)
        scratch = []
    else:
        in_specs.append(pl.BlockSpec(whole, lambda n, o: (0, 0, 0)))
        args.append(begun)
        out_specs = pl.BlockSpec((tokens, 2 * rows), lambda n, o: (0, 0))
        out_shape = jax.ShapeDtypeStruct((tokens, 2 * rows), BF16)
        scratch = [pltpu.VMEM(whole, F32)]
    return pl.pallas_call(
        begin_kernel if begun is None else end_kernel,
        grid_spec=pltpu.PrefetchScalarGridSpec(
            num_scalar_prefetch=1, grid=(steps,), in_specs=in_specs, out_specs=out_specs, scratch_shapes=scratch
        ),
        out_shape=out_shape,
        compiler_params=pltpu.CompilerParams(vmem_limit_bytes=40 * 2**20),
        cost_estimate=pl.CostEstimate(
            flops=2 * steps * tokens * k * rows, bytes_accessed=2 * steps * k * (tokens + rows), transcendentals=0
        ),
        name="input_products",
    )(order, *args)


def tie_kernel(*refs):
    pass


def tie(value, *after):
    spec = pl.BlockSpec(memory_space=pl.ANY)
    return pl.pallas_call(
        tie_kernel,
        in_specs=[spec] * (1 + len(after)),
        out_specs=spec,
        out_shape=jax.ShapeDtypeStruct(value.shape, value.dtype),
        input_output_aliases={0: 0},
        cost_estimate=pl.CostEstimate(flops=1, bytes_accessed=1, transcendentals=0),
        name="tie",
    )(value, *after)


def halves_kernel(up_ref, down_ref, ahead_ref, back_ref):
    ahead_ref[...] = up_ref[...]
    back_ref[...] = down_ref[...]


def far_halves(up, down):
    block = (1,) + up.shape[1:]
    half = jax.ShapeDtypeStruct((2,) + up.shape[1:], up.dtype)
    return pl.pallas_call(
        halves_kernel,
        grid=(2,),
        in_specs=[pl.BlockSpec(block, lambda n: (n, 0, 0)), pl.BlockSpec(block, lambda n: (n + 2, 0, 0))],
        out_specs=[pl.BlockSpec(block, lambda n: (n, 0, 0))] * 2,
        out_shape=[half, half],
        cost_estimate=pl.CostEstimate(flops=1, bytes_accessed=1, transcendentals=0),
        name="far_halves",
    )(up, down)


def per_device(x_in, g, w):
    dp = lax.axis_index("dp")
    t = lax.axis_index("tensor")
    table = tables()
    order = lax.dynamic_index_in_dim(jnp.asarray(table), dp * NY * 2 + t, 0, keepdims=False)

    turned = send(w, TURN)
    plus, peak_a = weight_products(order, W_BASE, 1, x_in, g)
    turned = tie(turned, peak_a)
    near = [turned, send(turned, FIRST[1]), send(turned, FIRST[-1]), send(turned, FIRST[2])]
    minus, peak_b = weight_products(order, W_BASE + 4, 1, x_in, g)
    low, high, peak_c = weight_products(order, W_BASE + 8, 2, x_in, g)
    near[3] = tie(near[3], peak_c)

    g_all = lax.all_gather(g, "tensor", axis=0)

    line = jnp.stack(near)
    up, down = send(line, SECOND[1]), send(line, SECOND[-1])
    u, v = send(plus, FIRST[1]), send(minus, FIRST[-1])

    peaks = lax.all_gather(jnp.maximum(jnp.maximum(peak_a, peak_b), peak_c), AXES)
    u = tie(u, up, down)

    ahead, back = far_halves(up, down)
    far = [send(ahead, SECOND[1]), send(back, SECOND[-1])]
    r = send(add(low[0:2], u[0:2]).astype(BF16), FIRST[1])
    s = send(add(low[2:4], v[0:2]).astype(BF16), FIRST[-1])
    begun = input_products(order, g_all, [line, up, down])
    r = tie(r, begun)

    e = [add(high[0], v[2], r[0]), add(high[1], v[3], r[1]), add(high[2], u[2], s[0]), add(high[3], u[3], s[1])]
    e = [b.astype(BF16) for b in e]
    h = e[0].shape[0] // 2
    u = send(jnp.stack([e[2][:h], e[1][h:]]), SECOND[1])
    v = send(jnp.stack([e[2][h:], e[3][:h]]), SECOND[-1])
    grad_peak = jnp.max(peaks)
    input_grad = input_products(order, g_all, far, begun)
    u = tie(u, input_grad, peaks)
    r = send(add(e[1][:h], u[0]).astype(BF16), SECOND[1])
    s = send(add(e[3][h:], v[0]).astype(BF16), SECOND[-1])
    total = jnp.concatenate([add(e[0][:h], v[1], r), add(e[0][h:], u[1], s)], axis=0)
    weight_grad = total.T / grad_peak
    return input_grad, weight_grad, grad_peak


def solution(mesh):
    return jax.shard_map(
        per_device,
        mesh=mesh,
        in_specs=(P("dp", None), P("dp", "tensor"), P("dp", "tensor")),
        out_specs=(P("dp", "tensor"), P("dp", "tensor"), P()),
        check_vma=False,
    )
```
